32 devices in a mesh: grp: 4 (over y, x), dev: 8 (over z, core).
Axes of the slice: x: 2, y: 2, z: 4, core: 2. Of those that a mesh axis runs over, the one named last changes fastest.
Arguments:
- embeddings: bfloat16 [32768, 1024], P(('grp', 'dev')), may hold values from -6 to 6
- cluster_ids: int32 [32768, 1], P(('grp', 'dev')), may hold values from 0 to 255; in each aligned block of 1024 rows (0 to 1023, 1024 to 2047, ...) at most 8 rows name the same one
- cluster_slot: int32 [256], replicated, may hold values from 0 to 255, each once
Outputs:
- max_cosine: float32 [32768], P(('grp', 'dev'))
- centroids: float32 [256, 1024], P(('grp', 'dev'))
The draws below stay inside these ranges and needn't reach their ends.
All inputs are finite; a program needn't handle non-finite values.
Results may differ from the reference program's by a relative error of at most 0.0029.
Values may be sent and summed in bfloat16 or wider, within the bound.
A program may use at most 128 MiB of HBM per device.

```python
import math
import jax
import jax.numpy as jnp
import numpy as np
from jax import lax

D = 1024
MOST = 8
CLUSTERS = 256
ROWS_DEV = 1024
ROWS = 32768
SPAN = 256
N_GRP = 4
N_DEV = 8


def levels(key, dims, split, low, largest):
    gain, own = 1.0, jax.random.fold_in(key, 6)
    for dim, shards_of in split:
        draws = jnp.exp(jax.random.uniform(jax.random.fold_in(own, dim), (shards_of,), jnp.float32, low / len(split), largest / len(split)))
        gain = gain * jnp.repeat(draws, dims[dim] // shards_of).reshape([-1 if axis == dim else 1 for axis in range(len(dims))])
    return gain


def routed_block(stream_key, own, number, rows, number_of, top, bound, skew):
    sequence = jax.random.permutation(stream_key, number_of)
    packed, common = load_shares(number_of, rows * top, bound, skew, True), load_shares(number_of, rows * top, bound, skew, False)
    places = jnp.arange(number_of)

    def named(tallies, rotation):
        used = int((tallies > 0).sum())
        fixed = max(1, used // 4)
        passed = fixed + (places - fixed + rotation * (used - fixed)) % max(1, number_of - fixed)
        return jnp.zeros((number_of,), jnp.int32).at[sequence[jnp.where(places < fixed, places, passed)]].set(jnp.asarray(tallies, jnp.int32))

    tallies = jnp.where(number % 4 == 0, named(packed, number // 4), named(common, number - number // 4 - 1))
    mixed = jax.random.permutation(jax.random.fold_in(own, 3), number_of)
    donor, receiver = mixed[0:number_of // 2 * 2:2], mixed[1:number_of // 2 * 2:2]
    margin = jnp.minimum(tallies[donor] - 1, bound - tallies[receiver]) // 2
    margin = jnp.where((donor == sequence[0]) | (receiver == sequence[0]) | (tallies[receiver] == 0), 0, jnp.maximum(margin, 0))
    passed = jax.random.randint(jax.random.fold_in(own, 4), (number_of // 2,), 0, 1 << 20) % (margin + 1)
    tallies = tallies.at[donor].add(-passed).at[receiver].add(passed)
    labels = jnp.searchsorted(jnp.cumsum(tallies), jnp.arange(rows * top), side="right").astype(jnp.int32)
    grid = labels.reshape(top, rows).T
    grid = grid[jax.random.permutation(jax.random.fold_in(own, 1), rows)]
    rotation = jax.random.randint(jax.random.fold_in(own, 2), (rows, 1), 0, top)
    return jnp.take_along_axis(grid, (jnp.arange(top)[None, :] + rotation) % top, axis=1)


def load_shares(amount, total, bound, skew, full):
    weights = [(1 << 20) // math.isqrt(grade ** skew) + 1 for grade in range(1, amount + 1)]
    largest = bound if full else min(bound, max(-(-total // amount), total * weights[0] // sum(weights)))
    least = 1 if total - largest >= amount - 1 else 0
    holding, spare = [largest] + [least] * (amount - 1), total - largest - least * (amount - 1)
    while spare > 0:
        movable = [i for i in range(1, amount) if holding[i] < largest] or [i for i in range(1, amount) if holding[i] < bound]
        whole, remaining = sum([weights[i] for i in movable]), spare
        for i in movable:
            more = min(bound - holding[i], max(1, remaining * weights[i] // whole), spare)
            holding[i] = holding[i] + more
            spare = spare - more
    return np.array(holding)


def centred(own_key, extent, deviation, reach, split=(), kind=jnp.bfloat16):
    result = jax.random.normal(own_key, extent, jnp.float32) * deviation
    if len(split) > 0:
        result = levels(own_key, extent, split, -0.22, 0.18) * result
    return jnp.clip(result, min=-reach, max=reach).astype(kind)


def setup_inputs(seed: int = 0) -> dict:
    arg_keys = jax.random.split(jax.random.key(seed), 4)
    embeddings = centred(arg_keys[0], (ROWS, D), 1.0, 6.0, ((0, 32),))
    cluster_ids_keys = jax.random.split(jax.random.fold_in(arg_keys[1], 1), ROWS // ROWS_DEV)
    cluster_ids_turns = jax.random.permutation(jax.random.fold_in(arg_keys[1], 3), ROWS // ROWS_DEV)
    cluster_ids = jax.vmap(lambda own, number: routed_block(jax.random.fold_in(arg_keys[1], 2), own, number, ROWS_DEV, CLUSTERS, 1, MOST, 2))(cluster_ids_keys, cluster_ids_turns).reshape((ROWS, 1))
    cluster_slot = jax.random.permutation(arg_keys[2], CLUSTERS).astype(jnp.int32)
    return dict(embeddings=embeddings, cluster_ids=cluster_ids, cluster_slot=cluster_slot)


def reference(embeddings, cluster_ids, cluster_slot):
    ndev = N_GRP * N_DEV
    emb32 = embeddings.astype(jnp.float32)
    normalized = (emb32 / jnp.sqrt(lax.optimization_barrier(jnp.sum(emb32 * emb32, axis=1, keepdims=True)) + 1e-06)).astype(jnp.bfloat16)
    ids = cluster_ids[:, 0].astype(jnp.int32)
    ids_dev = ids.reshape(ndev, ROWS_DEV)
    order = jnp.arange(ROWS_DEV, dtype=jnp.int32)

    def rank_of(block):
        same = (block[:, None] == block[None, :]) & (order[None, :] < order[:, None])
        return lax.optimization_barrier(jnp.sum(same.astype(jnp.int32), axis=1))
    ranks = lax.map(rank_of, ids_dev).reshape(-1)
    source = jnp.repeat(jnp.arange(ndev, dtype=jnp.int32), ROWS_DEV)
    slots = cluster_slot[ids]
    position = slots * SPAN + source * MOST + ranks
    table = jnp.full((CLUSTERS * SPAN,), -1, jnp.int32).at[position].set(jnp.arange(ROWS, dtype=jnp.int32))
    table = table.reshape(CLUSTERS, SPAN)

    def per_cluster(members):
        valid = members >= 0
        rows = normalized[jnp.maximum(members, 0)]
        gram = jnp.dot(rows, rows.T, preferred_element_type=jnp.float32)
        keep = valid[None, :] & ~jnp.eye(SPAN, dtype=bool)
        return lax.optimization_barrier(jnp.max(jnp.where(keep, gram, -1.0), axis=1))
    maxima = lax.map(per_cluster, table).reshape(-1)
    max_cosine = maxima[position]
    sums = jax.ops.segment_sum(normalized.astype(jnp.float32), slots, num_segments=CLUSTERS)
    centroids = sums / jnp.sqrt(lax.optimization_barrier(jnp.sum(sums * sums, axis=1, keepdims=True)) + 1e-06)
    return (max_cosine, centroids)
```

```python
import functools

import jax
import jax.numpy as jnp
from jax import lax
from jax.experimental import pallas as pl
from jax.experimental.pallas import tpu as pltpu
from jax.sharding import PartitionSpec as P

MOST = 8
MESH = pl.DeviceIdType.MESH
F32 = jnp.float32
BF16 = jnp.bfloat16
CHUNK = 256


def iota(shape, dim):
    return lax.broadcasted_iota(jnp.int32, shape, dim)


def kernel(
    n_grp,
    n_dev,
    owned,
    quota,
    group,
    emb,
    ids,
    slot_row,
    best_out,
    cent_out,
    norm,
    send,
    recv,
    where_row,
    lab_mat,
    lab_send,
    lab_recv,
    lab_rows,
    lab_cols,
    best,
    ret_send,
    ret_recv,
    ret_mat,
    sums,
    load_sem,
    send_sem,
    recv_sem,
    small_send,
    small_recv,
):
    n = n_grp * n_dev
    rows = norm.shape[0]
    clusters = slot_row.shape[1]
    span = group * quota
    n_groups = n // group
    my_g = lax.axis_index("grp")
    my_d = lax.axis_index("dev")

    def ahead(k):
        return (my_g + k // n_dev) % n_grp, (my_d + k % n_dev) % n_dev

    def behind(k):
        return (my_g + n_grp - k // n_dev) % n_grp, (my_d + n_dev - k % n_dev) % n_dev

    barrier = pltpu.get_barrier_semaphore()

    @pl.loop(1, n)
    def _(k):
        pl.semaphore_signal(barrier, inc=1, device_id=ahead(k), device_id_type=MESH)

    def load(c):
        part = pl.ds(pl.multiple_of(c * CHUNK, CHUNK), CHUNK)
        return pltpu.make_async_copy(emb.at[part], norm.at[part], load_sem.at[c])

    @pl.loop(0, rows // CHUNK)
    def _(c):
        load(c).start()

    eye = iota((clusters, clusters), 0) == iota((clusters, clusters), 1)
    slot_col = jnp.sum(jnp.where(eye, slot_row[...].astype(F32), 0.0), axis=1, keepdims=True)

    lab_mat[...] = jnp.zeros_like(lab_mat)
    before = (iota((CHUNK, CHUNK), 0) < iota((CHUNK, CHUNK), 1)).astype(BF16)
    grp_f = my_g.astype(F32)
    dev_f = my_d.astype(F32)

    def place(c, carry):
        part = pl.ds(pl.multiple_of(c * CHUNK, CHUNK), CHUNK)
        hit = iota((clusters, CHUNK), 0) == ids[:, part]
        slot = jnp.sum(jnp.where(hit, slot_col, 0.0), axis=0, keepdims=True)
        owner = jnp.floor((slot + 0.5) * (1.0 / owned))
        local = slot - owner * owned
        og = jnp.floor((owner + 0.5) * (1.0 / n_dev))
        kg = og - grp_f
        kd = owner - og * n_dev - dev_f
        kg = jnp.where(kg < 0, kg + n_grp, kg)
        kd = jnp.where(kd < 0, kd + n_dev, kd)
        k = kg * n_dev + kd
        mine = iota((n, CHUNK), 0).astype(F32) == k
        hot = mine.astype(F32)
        earlier = jnp.dot(hot.astype(BF16), before, preferred_element_type=F32) + carry
        pos = jnp.sum(hot * earlier, axis=0, keepdims=True)
        gk = jnp.floor((k + 0.5) * (1.0 / group))
        lane = (k - gk * group) * quota + pos
        where_row[0:1, part] = k
        where_row[1:2, part] = lane
        where_row[2:3, part] = k * quota + pos
        spot = (iota((span, CHUNK), 0).astype(F32) == lane).astype(BF16)
        lab_mat[...] += lax.dot_general(
            (hot * (local + 1.0)).astype(BF16),
            spot,
            (((1,), (1,)), ((), ())),
            preferred_element_type=F32,
        )
        return carry + jnp.sum(hot, axis=1, keepdims=True)

    lax.fori_loop(0, rows // CHUNK, place, jnp.zeros((n, 1), F32))

    pl.semaphore_wait(barrier, n - 1)

    lab_recv[0] = lab_mat[0:1, :]

    @pl.loop(1, n)
    def _(k):
        lab_send[k] = lab_mat[pl.ds(k, 1), :]
        pltpu.make_async_remote_copy(
            src_ref=lab_send.at[k],
            dst_ref=lab_recv.at[k],
            send_sem=small_send.at[0],
            recv_sem=small_recv.at[0],
            device_id=ahead(k),
            device_id_type=MESH,
        ).start()

    @pl.loop(0, rows // CHUNK)
    def _(c):
        load(c).wait()
        part = pl.ds(pl.multiple_of(c * CHUNK, CHUNK), CHUNK)
        x = norm[part, :].astype(F32)
        norm[part, :] = (x * lax.rsqrt(jnp.sum(x * x, axis=1, keepdims=True) + 1e-06)).astype(BF16)

    @pl.loop(0, n_groups)
    def _(g):
        spots = (iota((span, rows), 0) + g * span).astype(F32) == where_row[2:3, :]
        block = jnp.dot(spots.astype(BF16), norm[...], preferred_element_type=F32).astype(BF16)
        send[pl.ds(pl.multiple_of(g * span, span), span), :] = block

        @pl.when(g == 0)
        def _():
            recv[0:quota, :] = block[0:quota]

        @pl.loop(0, group)
        def _(j):
            k = g * group + j

            @pl.when(k > 0)
            def _():
                part = pl.ds(pl.multiple_of(k * quota, quota), quota)
                pltpu.make_async_remote_copy(
                    src_ref=send.at[part],
                    dst_ref=recv.at[part],
                    send_sem=send_sem,
                    recv_sem=recv_sem.at[g],
                    device_id=ahead(k),
                    device_id_type=MESH,
                ).start()

    others = lab_recv.at[pl.ds(1, n - 1)]
    pltpu.make_async_copy(others, others, small_recv.at[0]).wait()
    diag = iota((span, span), 0) == iota((span, span), 1)

    @pl.loop(0, n_groups)
    def _(g):
        row = lab_recv[g * group]
        for j in range(1, group):
            row = row + lab_recv[g * group + j]
        lab_rows[g] = row
        lab_cols[g] = jnp.sum(jnp.where(diag, row, 0.0), axis=1, keepdims=True)
        best[g] = jnp.full((1, span), -1.0, F32)

    sums[...] = jnp.zeros_like(sums)

    def contract(a, b):
        return lax.dot_general(a, b, (((1,), (1,)), ((), ())), preferred_element_type=F32)

    @pl.loop(0, n_groups)
    def _(g):
        @pl.when(g == 0)
        def _():
            got = recv.at[pl.ds(quota, span - quota)]
            pltpu.make_async_copy(got, got, recv_sem.at[0]).wait()

        @pl.when(g > 0)
        def _():
            got = recv.at[pl.ds(pl.multiple_of(g * span, span), span)]
            pltpu.make_async_copy(got, got, recv_sem.at[g]).wait()

        new = recv[pl.ds(pl.multiple_of(g * span, span), span), :]
        member = iota((owned, span), 0).astype(F32) + 1.0 == lab_rows[g]
        sums[...] += jnp.dot(member.astype(BF16), new, preferred_element_type=F32)

        keep = (lab_cols[g] == lab_rows[g]) & ~diag
        top = jnp.max(jnp.where(keep, contract(new, new), -1.0), axis=0, keepdims=True)
        best[g] = jnp.maximum(best[g], top)

        @pl.loop(0, g)
        def _(h):
            old = recv[pl.ds(pl.multiple_of(h * span, span), span), :]
            keep = lab_cols[h] == lab_rows[g]
            top = jnp.max(jnp.where(keep, contract(old, new), -1.0), axis=0, keepdims=True)
            best[g] = jnp.maximum(best[g], top)
            keep = lab_cols[g] == lab_rows[h]
            top = jnp.max(jnp.where(keep, contract(new, old), -1.0), axis=0, keepdims=True)
            best[h] = jnp.maximum(best[h], top)

    ret_recv[0] = best[0]

    @pl.loop(1, n)
    def _(k):
        ret_send[k] = best[k // group]
        pltpu.make_async_remote_copy(
            src_ref=ret_send.at[k],
            dst_ref=ret_recv.at[k],
            send_sem=small_send.at[1],
            recv_sem=small_recv.at[1],
            device_id=behind(k),
            device_id_type=MESH,
        ).start()

    total = sums[...]
    cent_out[...] = total * lax.rsqrt(jnp.sum(total * total, axis=1, keepdims=True) + 1e-06)

    back = ret_recv.at[pl.ds(1, n - 1)]
    pltpu.make_async_copy(back, back, small_recv.at[1]).wait()

    @pl.loop(0, n)
    def _(k):
        ret_mat[pl.ds(k, 1), :] = ret_recv[k]

    @pl.loop(0, rows // CHUNK)
    def _(c):
        part = pl.ds(pl.multiple_of(c * CHUNK, CHUNK), CHUNK)
        hot = (iota((n, CHUNK), 0).astype(F32) == where_row[0:1, part]).astype(F32)
        picked = lax.dot_general(
            ret_mat[...],
            hot,
            (((0,), (0,)), ((), ())),
            precision=lax.Precision.HIGHEST,
            preferred_element_type=F32,
        )
        spot = iota((span, CHUNK), 0).astype(F32) == where_row[1:2, part]
        best_out[:, part] = jnp.sum(jnp.where(spot, picked, 0.0), axis=0, keepdims=True)

    sent = send.at[pl.ds(quota, n * quota - quota)]
    pltpu.make_async_copy(sent, sent, send_sem).wait()
    sent = lab_send.at[pl.ds(1, n - 1)]
    pltpu.make_async_copy(sent, sent, small_send.at[0]).wait()
    sent = ret_send.at[pl.ds(1, n - 1)]
    pltpu.make_async_copy(sent, sent, small_send.at[1]).wait()


def local(embeddings, cluster_ids, cluster_slot):
    n_grp = lax.axis_size("grp")
    n_dev = lax.axis_size("dev")
    n = n_grp * n_dev
    rows, width = embeddings.shape
    clusters = cluster_slot.shape[0]
    owned = clusters // n
    quota = owned * MOST
    group = 4
    span = group * quota
    groups = n // group
    vmem = pl.BlockSpec(memory_space=pltpu.VMEM)
    best, cent = pl.pallas_call(
        functools.partial(kernel, n_grp, n_dev, owned, quota, group),
        out_shape=(
            jax.ShapeDtypeStruct((1, rows), F32),
            jax.ShapeDtypeStruct((owned, width), F32),
        ),
        in_specs=[pl.BlockSpec(memory_space=pl.ANY), vmem, vmem],
        out_specs=(vmem, vmem),
        scratch_shapes=[
            pltpu.VMEM((rows, width), BF16),
            pltpu.VMEM((n * quota, width), BF16),
            pltpu.VMEM((n * quota, width), BF16),
            pltpu.VMEM((8, rows), F32),
            pltpu.VMEM((n, span), F32),
            pltpu.VMEM((n, 1, span), F32),
            pltpu.VMEM((n, 1, span), F32),
            pltpu.VMEM((groups, 1, span), F32),
            pltpu.VMEM((groups, span, 1), F32),
            pltpu.VMEM((groups, 1, span), F32),
            pltpu.VMEM((n, 1, span), F32),
            pltpu.VMEM((n, 1, span), F32),
            pltpu.VMEM((n, span), F32),
            pltpu.VMEM((owned, width), F32),
            pltpu.SemaphoreType.DMA((rows // CHUNK,)),
            pltpu.SemaphoreType.DMA,
            pltpu.SemaphoreType.DMA((groups,)),
            pltpu.SemaphoreType.DMA((2,)),
            pltpu.SemaphoreType.DMA((2,)),
        ],
        compiler_params=pltpu.CompilerParams(
            collective_id=0, has_side_effects=True, vmem_limit_bytes=60 * 1024 * 1024
        ),
    )(embeddings, cluster_ids.reshape(1, rows), cluster_slot.reshape(1, clusters))
    return best.reshape(rows), cent


def solution(mesh):
    in_specs = (P(("grp", "dev"), None), P(("grp", "dev"), None), P())
    out_specs = (P(("grp", "dev")), P(("grp", "dev"), None))
    return jax.shard_map(local, mesh=mesh, in_specs=in_specs, out_specs=out_specs, check_vma=False)
```

```python
import functools

import jax
import jax.numpy as jnp
from jax import lax
from jax.experimental import pallas as pl
from jax.experimental.pallas import tpu as pltpu
from jax.sharding import PartitionSpec as P

MOST = 8
CORES = 2
MESH = pl.DeviceIdType.MESH
F32 = jnp.float32
BF16 = jnp.bfloat16
CHUNK = 256


def iota(shape, dim):
    return lax.broadcasted_iota(jnp.int32, shape, dim)


def iotaf(shape, dim):
    return iota(shape, dim).astype(F32)


def floordiv(x, by):
    return jnp.floor((x + 0.5) * (1.0 / by))


def kernel(
    n_grp,
    n_z,
    owned,
    quota,
    part,
    group,
    emb,
    ids,
    slot_row,
    best_out,
    cent_out,
    flag_out,
    norm,
    send,
    recv,
    where_row,
    lab_mat,
    lab_send,
    lab_recv,
    lab_rows,
    lab_cols,
    best,
    ret_send,
    ret_recv,
    ret_mat,
    sums,
    load_sem,
    send_sem,
    recv_sem,
    pass_send,
    pass_recv,
    small_send,
    small_recv,
):
    chips = n_grp * n_z
    n = chips * CORES
    pair = 2 * part
    over = quota - part
    rows = norm.shape[0]
    clusters = slot_row.shape[1]
    span = group * quota
    n_groups = n // group
    group_chips = group // CORES
    my_g = lax.axis_index("grp")
    my_d = lax.axis_index("dev")
    my_z = my_d // CORES
    my_c = my_d % CORES

    def ahead(k):
        chip = k // CORES
        return (my_g + chip // n_z) % n_grp, ((my_z + chip % n_z) % n_z) * CORES + k % CORES

    def behind(k):
        chip = k // CORES
        return (
            (my_g + n_grp - chip // n_z) % n_grp,
            ((my_z + n_z - chip % n_z) % n_z) * CORES + k % CORES,
        )

    barrier = pltpu.get_barrier_semaphore()

    @pl.loop(0, n)
    def _(k):
        @pl.when(k != my_c)
        def _():
            pl.semaphore_signal(barrier, inc=1, device_id=ahead(k), device_id_type=MESH)

    def load(c):
        at = pl.ds(pl.multiple_of(c * CHUNK, CHUNK), CHUNK)
        return pltpu.make_async_copy(emb.at[at], norm.at[at], load_sem.at[c])

    @pl.loop(0, rows // CHUNK)
    def _(c):
        load(c).start()

    eye = iota((clusters, clusters), 0) == iota((clusters, clusters), 1)
    slot_col = jnp.sum(jnp.where(eye, slot_row[...].astype(F32), 0.0), axis=1, keepdims=True)

    lab_mat[...] = jnp.zeros_like(lab_mat)
    before = (iota((CHUNK, CHUNK), 0) < iota((CHUNK, CHUNK), 1)).astype(BF16)
    grp_f = my_g.astype(F32)
    z_f = my_z.astype(F32)
    core_f = my_c.astype(F32)

    def place(c, carry):
        count, filled = carry
        at = pl.ds(pl.multiple_of(c * CHUNK, CHUNK), CHUNK)
        hit = iota((clusters, CHUNK), 0) == ids[:, at]
        slot = jnp.sum(jnp.where(hit, slot_col, 0.0), axis=0, keepdims=True)
        owner = floordiv(slot, owned)
        local = slot - owner * owned
        owner_chip = floordiv(owner, CORES)
        core = owner - owner_chip * CORES
        owner_grp = floordiv(owner_chip, n_z)
        kg = owner_grp - grp_f
        kz = owner_chip - owner_grp * n_z - z_f
        kg = jnp.where(kg < 0, kg + n_grp, kg)
        kz = jnp.where(kz < 0, kz + n_z, kz)
        chip = kg * n_z + kz
        k = chip * CORES + core
        hot = (iotaf((n, CHUNK), 0) == k).astype(F32)
        earlier = jnp.dot(hot.astype(BF16), before, preferred_element_type=F32) + count
        pos = jnp.sum(hot * earlier, axis=0, keepdims=True)
        line = jnp.where(core > 0, quota - 1 - pos, pos)
        in_group = chip - floordiv(chip, group_chips) * group_chips
        lane = (in_group * CORES + core_f) * quota + line
        where_row[0:1, at] = k
        where_row[1:2, at] = lane
        where_row[2:3, at] = chip * pair + core * (pair - quota) + line
        spot = (iotaf((span, CHUNK), 0) == lane).astype(BF16)
        lab_mat[:, 0:span] += lax.dot_general(
            (hot * (local + 1.0)).astype(BF16),
            spot,
            (((1,), (1,)), ((), ())),
            preferred_element_type=F32,
        )
        count = count + jnp.sum(hot, axis=1, keepdims=True)
        to_chip = (iotaf((chips, CHUNK), 0) == chip).astype(F32)
        return count, filled + jnp.sum(to_chip, axis=1, keepdims=True)

    _, filled = lax.fori_loop(
        0, rows // CHUNK, place, (jnp.zeros((n, 1), F32), jnp.zeros((chips, 1), F32))
    )
    crowded = jnp.max((filled > pair).astype(F32), axis=0, keepdims=True)
    lab_mat[:, span:] = jnp.broadcast_to(crowded, (n, lab_mat.shape[1] - span))

    pl.semaphore_wait(barrier, n - 1)

    lab_recv[my_c] = lab_mat[pl.ds(my_c, 1), :]

    @pl.loop(0, n)
    def _(k):
        @pl.when(k != my_c)
        def _():
            lab_send[k] = lab_mat[pl.ds(k, 1), :]
            pltpu.make_async_remote_copy(
                src_ref=lab_send.at[k],
                dst_ref=lab_recv.at[(k // CORES) * CORES + my_c],
                send_sem=small_send.at[0],
                recv_sem=small_recv.at[0],
                device_id=ahead(k),
                device_id_type=MESH,
            ).start()

    @pl.loop(0, rows // CHUNK)
    def _(c):
        load(c).wait()
        at = pl.ds(pl.multiple_of(c * CHUNK, CHUNK), CHUNK)
        x = norm[at, :].astype(F32)
        norm[at, :] = (x * lax.rsqrt(jnp.sum(x * x, axis=1, keepdims=True) + 1e-06)).astype(BF16)

    made = group_chips * pair

    @pl.loop(0, n_groups)
    def _(g):
        spots = (iota((made, rows), 0) + g * made).astype(F32) == where_row[2:3, :]
        block = jnp.dot(spots.astype(BF16), norm[...], preferred_element_type=F32).astype(BF16)
        send[pl.ds(pl.multiple_of(g * made, made), made), :] = block

        @pl.when(g == 0)
        def _():
            own = send[pl.ds(pl.multiple_of(my_c * part, 16), part), :]
            recv[pl.ds(pl.multiple_of(my_c * (quota + over), 16), part), :] = own

        @pl.loop(0, group)
        def _(j):
            k = g * group + j
            core = k % CORES

            @pl.when(k != my_c)
            def _():
                to = ((k // CORES) * CORES + my_c) * quota + core * over
                pltpu.make_async_remote_copy(
                    src_ref=send.at[pl.ds(pl.multiple_of(k * part, 16), part)],
                    dst_ref=recv.at[pl.ds(pl.multiple_of(to, 16), part)],
                    send_sem=send_sem,
                    recv_sem=recv_sem.at[g],
                    device_id=ahead(k),
                    device_id_type=MESH,
                ).start()

    others = lab_recv.at[pl.ds(1, n - 1)]
    pltpu.make_async_copy(others, others, small_recv.at[0]).wait()
    diag = iota((span, span), 0) == iota((span, span), 1)
    flag_out[...] = jnp.zeros_like(flag_out)

    @pl.loop(0, n_groups)
    def _(g):
        row = lab_recv[g * group]
        for j in range(1, group):
            row = row + lab_recv[g * group + j]
        lab_rows[g] = row[:, 0:span]
        lab_cols[g] = jnp.sum(jnp.where(diag, row[:, 0:span], 0.0), axis=1, keepdims=True)
        best[g] = jnp.full((1, span), -1.0, F32)
        flag_out[...] += row[:, span:]

    sums[...] = jnp.zeros_like(sums)

    def contract(a, b):
        return lax.dot_general(a, b, (((1,), (1,)), ((), ())), preferred_element_type=F32)

    def arrive(g):
        @pl.when(g == 0)
        def _():
            got = recv.at[pl.ds(0, (group - 1) * part)]
            pltpu.make_async_copy(got, got, recv_sem.at[0]).wait()

        @pl.when(g > 0)
        def _():
            got = recv.at[pl.ds(pl.multiple_of(g * span, span), group * part)]
            pltpu.make_async_copy(got, got, recv_sem.at[g]).wait()

        if over:
            @pl.loop(0, group)
            def _(j):
                base = (g * group + j) * quota
                start = base + (pair - quota) - my_c * (pair - quota - over)
                to = base + my_c * part
                pltpu.make_async_remote_copy(
                    src_ref=recv.at[pl.ds(pl.multiple_of(start, 16), over)],
                    dst_ref=recv.at[pl.ds(pl.multiple_of(to, 16), over)],
                    send_sem=pass_send,
                    recv_sem=pass_recv.at[g],
                    device_id=(my_g, my_z * CORES + (1 - my_c)),
                    device_id_type=MESH,
                ).start()

    def compare(g):
        if over:
            got = recv.at[pl.ds(pl.multiple_of(g * span, span), group * over)]
            pltpu.make_async_copy(got, got, pass_recv.at[g]).wait()
        new = recv[pl.ds(pl.multiple_of(g * span, span), span), :]
        member = iotaf((owned, span), 0) + 1.0 == lab_rows[g]
        sums[...] += jnp.dot(member.astype(BF16), new, preferred_element_type=F32)

        keep = (lab_cols[g] == lab_rows[g]) & ~diag
        top = jnp.max(jnp.where(keep, contract(new, new), -1.0), axis=0, keepdims=True)
        best[g] = jnp.maximum(best[g], top)

        @pl.loop(0, g)
        def _(h):
            old = recv[pl.ds(pl.multiple_of(h * span, span), span), :]
            keep = lab_cols[h] == lab_rows[g]
            top = jnp.max(jnp.where(keep, contract(old, new), -1.0), axis=0, keepdims=True)
            best[g] = jnp.maximum(best[g], top)
            keep = lab_cols[g] == lab_rows[h]
            top = jnp.max(jnp.where(keep, contract(new, old), -1.0), axis=0, keepdims=True)
            best[h] = jnp.maximum(best[h], top)

    @pl.loop(0, n_groups + 1)
    def _(g):
        @pl.when(g < n_groups)
        def _():
            arrive(g)

        @pl.when(g > 0)
        def _():
            compare(g - 1)

    ret_recv[my_c] = best[0]

    @pl.loop(0, n)
    def _(k):
        @pl.when(k != my_c)
        def _():
            ret_send[k] = best[k // group]
            pltpu.make_async_remote_copy(
                src_ref=ret_send.at[k],
                dst_ref=ret_recv.at[(k // CORES) * CORES + my_c],
                send_sem=small_send.at[1],
                recv_sem=small_recv.at[1],
                device_id=behind(k),
                device_id_type=MESH,
            ).start()

    total = sums[...]
    cent_out[...] = total * lax.rsqrt(jnp.sum(total * total, axis=1, keepdims=True) + 1e-06)

    back = ret_recv.at[pl.ds(1, n - 1)]
    pltpu.make_async_copy(back, back, small_recv.at[1]).wait()

    @pl.loop(0, n)
    def _(k):
        ret_mat[pl.ds(k, 1), :] = ret_recv[k]

    @pl.loop(0, rows // CHUNK)
    def _(c):
        at = pl.ds(pl.multiple_of(c * CHUNK, CHUNK), CHUNK)
        hot = (iotaf((n, CHUNK), 0) == where_row[0:1, at]).astype(F32)
        picked = lax.dot_general(
            ret_mat[...],
            hot,
            (((0,), (0,)), ((), ())),
            precision=lax.Precision.HIGHEST,
            preferred_element_type=F32,
        )
        spot = iotaf((span, CHUNK), 0) == where_row[1:2, at]
        best_out[:, at] = jnp.sum(jnp.where(spot, picked, 0.0), axis=0, keepdims=True)

    sent = send.at[pl.ds(part, n * part - part)]
    pltpu.make_async_copy(sent, sent, send_sem).wait()
    if over:
        sent = recv.at[pl.ds(0, n * over)]
        pltpu.make_async_copy(sent, sent, pass_send).wait()
    sent = lab_send.at[pl.ds(1, n - 1)]
    pltpu.make_async_copy(sent, sent, small_send.at[0]).wait()
    sent = ret_send.at[pl.ds(1, n - 1)]
    pltpu.make_async_copy(sent, sent, small_send.at[1]).wait()


def exchange(embeddings, ids, slot_row, part, number):
    n_grp = lax.axis_size("grp")
    n_z = lax.axis_size("dev") // CORES
    n = n_grp * n_z * CORES
    rows, width = embeddings.shape
    clusters = slot_row.shape[1]
    owned = clusters // n
    quota = owned * MOST
    group = 4
    span = group * quota
    groups = n // group
    vmem = pl.BlockSpec(memory_space=pltpu.VMEM)
    return pl.pallas_call(
        functools.partial(kernel, n_grp, n_z, owned, quota, part, group),
        out_shape=(
            jax.ShapeDtypeStruct((1, rows), F32),
            jax.ShapeDtypeStruct((owned, width), F32),
            jax.ShapeDtypeStruct((1, 128), F32),
        ),
        in_specs=[pl.BlockSpec(memory_space=pl.ANY), vmem, vmem],
        out_specs=(vmem, vmem, vmem),
        scratch_shapes=[
            pltpu.VMEM((rows, width), BF16),
            pltpu.VMEM((n * part, width), BF16),
            pltpu.VMEM((n * quota, width), BF16),
            pltpu.VMEM((8, rows), F32),
            pltpu.VMEM((n, span + 128), F32),
            pltpu.VMEM((n, 1, span + 128), F32),
            pltpu.VMEM((n, 1, span + 128), F32),
            pltpu.VMEM((groups, 1, span), F32),
            pltpu.VMEM((groups, span, 1), F32),
            pltpu.VMEM((groups, 1, span), F32),
            pltpu.VMEM((n, 1, span), F32),
            pltpu.VMEM((n, 1, span), F32),
            pltpu.VMEM((n, span), F32),
            pltpu.VMEM((owned, width), F32),
            pltpu.SemaphoreType.DMA((rows // CHUNK,)),
            pltpu.SemaphoreType.DMA,
            pltpu.SemaphoreType.DMA((groups,)),
            pltpu.SemaphoreType.DMA,
            pltpu.SemaphoreType.DMA((groups,)),
            pltpu.SemaphoreType.DMA((2,)),
            pltpu.SemaphoreType.DMA((2,)),
        ],
        compiler_params=pltpu.CompilerParams(
            collective_id=number, has_side_effects=True, vmem_limit_bytes=60 * 1024 * 1024
        ),
    )(embeddings, ids, slot_row)


def local(embeddings, cluster_ids, cluster_slot):
    rows = embeddings.shape[0]
    clusters = cluster_slot.shape[0]
    ids = cluster_ids.reshape(1, rows)
    slot_row = cluster_slot.reshape(1, clusters)
    quota = clusters // lax.axis_size(("grp", "dev")) * MOST
    best, cent, crowded = exchange(embeddings, ids, slot_row, quota * 3 // 4, 0)

    def whole():
        again = exchange(embeddings, ids, slot_row, quota, 1)
        return again[0], again[1]

    best, cent = lax.cond(crowded[0, 0] > 0, whole, lambda: (best, cent))
    return best.reshape(rows), cent


def solution(mesh):
    in_specs = (P(("grp", "dev"), None), P(("grp", "dev"), None), P())
    out_specs = (P(("grp", "dev")), P(("grp", "dev"), None))
    return jax.shard_map(local, mesh=mesh, in_specs=in_specs, out_specs=out_specs, check_vma=False)
```

```python
import functools

import jax
import jax.numpy as jnp
from jax import lax
from jax.experimental import pallas as pl
from jax.experimental.pallas import tpu as pltpu
from jax.sharding import PartitionSpec as P

MOST = 8
CORES = 2
MESH = pl.DeviceIdType.MESH
F32 = jnp.float32
BF16 = jnp.bfloat16
CHUNK = 256


def iota(shape, dim):
    return lax.broadcasted_iota(jnp.int32, shape, dim)


def iotaf(shape, dim):
    return iota(shape, dim).astype(F32)


def floordiv(x, by):
    return jnp.floor((x + 0.5) * (1.0 / by))


def kernel(
    n_grp,
    n_z,
    owned,
    quota,
    part,
    group,
    emb,
    ids,
    slot_row,
    best_out,
    cent_out,
    flag_out,
    norm,
    send,
    recv,
    where_row,
    lab_mat,
    lab_send,
    lab_recv,
    lab_rows,
    lab_cols,
    best,
    ret_recv,
    ret_mat,
    sums,
    load_sem,
    send_sem,
    recv_sem,
    pass_send,
    pass_recv,
    small_send,
    small_recv,
):
    chips = n_grp * n_z
    n = chips * CORES
    pair = 2 * part
    over = quota - part
    rows = norm.shape[0]
    clusters = slot_row.shape[1]
    span = group * quota
    n_groups = n // group
    group_chips = group // CORES
    my_g = lax.axis_index("grp")
    my_d = lax.axis_index("dev")
    my_z = lax.div(my_d, CORES)
    my_c = lax.rem(my_d, CORES)

    def ahead(k):
        chip, core = lax.div(k, CORES), lax.rem(k, CORES)
        to_g = lax.rem(my_g + lax.div(chip, n_z), n_grp)
        return to_g, lax.rem(my_z + chip, n_z) * CORES + core

    def behind(k):
        chip, core = lax.div(k, CORES), lax.rem(k, CORES)
        to_g = lax.rem(my_g + n_grp - lax.div(chip, n_z), n_grp)
        return to_g, lax.rem(my_z + n_z - lax.rem(chip, n_z), n_z) * CORES + core

    barrier = pltpu.get_barrier_semaphore()

    @pl.loop(0, n, unroll=8)
    def _(k):
        @pl.when(k != my_c)
        def _():
            pl.semaphore_signal(barrier, inc=1, device_id=ahead(k), device_id_type=MESH)

    def load(c):
        at = pl.ds(pl.multiple_of(c * CHUNK, CHUNK), CHUNK)
        return pltpu.make_async_copy(emb.at[at], norm.at[at], load_sem.at[c])

    @pl.loop(0, rows // CHUNK)
    def _(c):
        load(c).start()

    eye = iota((clusters, clusters), 0) == iota((clusters, clusters), 1)
    slot_col = jnp.sum(jnp.where(eye, slot_row[...].astype(F32), 0.0), axis=1, keepdims=True)

    lab_mat[...] = jnp.zeros_like(lab_mat)
    before = (iota((CHUNK, CHUNK), 0) < iota((CHUNK, CHUNK), 1)).astype(BF16)
    grp_f = my_g.astype(F32)
    z_f = my_z.astype(F32)
    core_f = my_c.astype(F32)

    def place(c, carry):
        count, filled = carry
        at = pl.ds(pl.multiple_of(c * CHUNK, CHUNK), CHUNK)
        hit = iota((clusters, CHUNK), 0) == ids[:, at]
        slot = jnp.sum(jnp.where(hit, slot_col, 0.0), axis=0, keepdims=True)
        owner = floordiv(slot, owned)
        local = slot - owner * owned
        owner_chip = floordiv(owner, CORES)
        core = owner - owner_chip * CORES
        owner_grp = floordiv(owner_chip, n_z)
        kg = owner_grp - grp_f
        kz = owner_chip - owner_grp * n_z - z_f
        kg = jnp.where(kg < 0, kg + n_grp, kg)
        kz = jnp.where(kz < 0, kz + n_z, kz)
        chip = kg * n_z + kz
        k = chip * CORES + core
        hot = (iotaf((n, CHUNK), 0) == k).astype(F32)
        earlier = jnp.dot(hot.astype(BF16), before, preferred_element_type=F32) + count
        pos = jnp.sum(hot * earlier, axis=0, keepdims=True)
        line = jnp.where(core > 0, quota - 1 - pos, pos)
        in_group = chip - floordiv(chip, group_chips) * group_chips
        lane = (in_group * CORES + core_f) * quota + line
        where_row[0:1, at] = k
        where_row[1:2, at] = lane
        where_row[2:3, at] = chip * pair + core * (pair - quota) + line
        spot = (iotaf((span, CHUNK), 0) == lane).astype(BF16)
        lab_mat[:, 0:span] += lax.dot_general(
            (hot * (local + 1.0)).astype(BF16),
            spot,
            (((1,), (1,)), ((), ())),
            preferred_element_type=F32,
        )
        count = count + jnp.sum(hot, axis=1, keepdims=True)
        to_chip = (iotaf((chips, CHUNK), 0) == chip).astype(F32)
        return count, filled + jnp.sum(to_chip, axis=1, keepdims=True)

    _, filled = lax.fori_loop(
        0, rows // CHUNK, place, (jnp.zeros((n, 1), F32), jnp.zeros((chips, 1), F32))
    )
    crowded = jnp.max((filled > pair).astype(F32), axis=0, keepdims=True)
    lab_mat[:, span:] = jnp.broadcast_to(crowded, (n, lab_mat.shape[1] - span))

    @pl.loop(0, rows // CHUNK)
    def _(c):
        load(c).wait()
        at = pl.ds(pl.multiple_of(c * CHUNK, CHUNK), CHUNK)
        x = norm[at, :].astype(F32)
        norm[at, :] = (x * lax.rsqrt(jnp.sum(x * x, axis=1, keepdims=True) + 1e-06)).astype(BF16)

    made = group_chips * pair

    def make(g):
        spots = (iota((made, rows), 0) + g * made).astype(F32) == where_row[2:3, :]
        block = jnp.dot(spots.astype(BF16), norm[...], preferred_element_type=F32).astype(BF16)
        send[pl.ds(pl.multiple_of(g * made, made), made), :] = block

    def ship(g):
        @pl.loop(0, group, unroll=True)
        def _(j):
            k = g * group + j
            twin = lax.div(k, CORES) * CORES + my_c

            @pl.when(k != my_c)
            def _():
                to = twin * quota + lax.rem(k, CORES) * over
                pltpu.make_async_remote_copy(
                    src_ref=send.at[pl.ds(pl.multiple_of(k * part, 16), part)],
                    dst_ref=recv.at[pl.ds(pl.multiple_of(to, 16), part)],
                    send_sem=send_sem,
                    recv_sem=recv_sem.at[g],
                    device_id=ahead(k),
                    device_id_type=MESH,
                ).start()

    make(0)
    own = send[pl.ds(pl.multiple_of(my_c * part, 16), part), :]
    recv[pl.ds(pl.multiple_of(my_c * (quota + over), 16), part), :] = own
    lab_recv[my_c] = lab_mat[pl.ds(my_c, 1), :]

    @pl.loop(0, n, unroll=8)
    def _(k):
        lab_send[k] = lab_mat[pl.ds(k, 1), :]

    pl.semaphore_wait(barrier, n - 1)
    ship(0)

    @pl.loop(1, n_groups)
    def _(g):
        make(g)
        ship(g)

        @pl.when(g == 1)
        def _():
            @pl.loop(0, n, unroll=8)
            def _(k):
                @pl.when(k != my_c)
                def _():
                    pltpu.make_async_remote_copy(
                        src_ref=lab_send.at[k],
                        dst_ref=lab_recv.at[lax.div(k, CORES) * CORES + my_c],
                        send_sem=small_send.at[0],
                        recv_sem=small_recv.at[0],
                        device_id=ahead(k),
                        device_id_type=MESH,
                    ).start()

    others = lab_recv.at[pl.ds(1, n - 1)]
    pltpu.make_async_copy(others, others, small_recv.at[0]).wait()
    diag = iota((span, span), 0) == iota((span, span), 1)
    flag_out[...] = jnp.zeros_like(flag_out)

    @pl.loop(0, n_groups)
    def _(g):
        row = lab_recv[g * group]
        for j in range(1, group):
            row = row + lab_recv[g * group + j]
        lab_rows[g] = row[:, 0:span]
        lab_cols[g] = jnp.sum(jnp.where(diag, row[:, 0:span], 0.0), axis=1, keepdims=True)
        best[g] = jnp.full((1, span), -1.0, F32)
        flag_out[...] += row[:, span:]

    sums[...] = jnp.zeros_like(sums)

    def contract(a, b):
        return lax.dot_general(a, b, (((1,), (1,)), ((), ())), preferred_element_type=F32)

    def arrive(g):
        @pl.when(g == 0)
        def _():
            got = recv.at[pl.ds(0, (group - 1) * part)]
            pltpu.make_async_copy(got, got, recv_sem.at[0]).wait()

        @pl.when(g > 0)
        def _():
            got = recv.at[pl.ds(pl.multiple_of(g * span, span), group * part)]
            pltpu.make_async_copy(got, got, recv_sem.at[g]).wait()

        if over:
            @pl.loop(0, group, unroll=True)
            def _(j):
                base = (g * group + j) * quota
                start = base + (pair - quota) - my_c * (pair - quota - over)
                to = base + my_c * part
                pltpu.make_async_remote_copy(
                    src_ref=recv.at[pl.ds(pl.multiple_of(start, 16), over)],
                    dst_ref=recv.at[pl.ds(pl.multiple_of(to, 16), over)],
                    send_sem=pass_send,
                    recv_sem=pass_recv.at[g],
                    device_id=(my_g, my_z * CORES + (1 - my_c)),
                    device_id_type=MESH,
                ).start()

    def compare(g):
        if over:
            got = recv.at[pl.ds(pl.multiple_of(g * span, span), group * over)]
            pltpu.make_async_copy(got, got, pass_recv.at[g]).wait()
        new = recv[pl.ds(pl.multiple_of(g * span, span), span), :]
        member = iotaf((owned, span), 0) + 1.0 == lab_rows[g]
        sums[...] += jnp.dot(member.astype(BF16), new, preferred_element_type=F32)

        keep = (lab_cols[g] == lab_rows[g]) & ~diag
        top = jnp.max(jnp.where(keep, contract(new, new), -1.0), axis=0, keepdims=True)
        best[g] = jnp.maximum(best[g], top)

        @pl.loop(0, g)
        def _(h):
            old = recv[pl.ds(pl.multiple_of(h * span, span), span), :]
            keep = lab_cols[h] == lab_rows[g]
            top = jnp.max(jnp.where(keep, contract(old, new), -1.0), axis=0, keepdims=True)
            best[g] = jnp.maximum(best[g], top)
            keep = lab_cols[g] == lab_rows[h]
            top = jnp.max(jnp.where(keep, contract(new, old), -1.0), axis=0, keepdims=True)
            best[h] = jnp.maximum(best[h], top)

    @pl.loop(0, n_groups)
    def _(g):
        arrive(g)
        compare(g)

    ret_recv[my_c] = best[0]

    @pl.loop(0, n, unroll=8)
    def _(k):
        @pl.when(k != my_c)
        def _():
            pltpu.make_async_remote_copy(
                src_ref=best.at[lax.div(k, group)],
                dst_ref=ret_recv.at[lax.div(k, CORES) * CORES + my_c],
                send_sem=small_send.at[1],
                recv_sem=small_recv.at[1],
                device_id=behind(k),
                device_id_type=MESH,
            ).start()

    total = sums[...]
    cent_out[...] = total * lax.rsqrt(jnp.sum(total * total, axis=1, keepdims=True) + 1e-06)

    back = ret_recv.at[pl.ds(1, n - 1)]
    pltpu.make_async_copy(back, back, small_recv.at[1]).wait()

    @pl.loop(0, n, unroll=8)
    def _(k):
        ret_mat[pl.ds(k, 1), :] = ret_recv[k]

    @pl.loop(0, rows // CHUNK)
    def _(c):
        at = pl.ds(pl.multiple_of(c * CHUNK, CHUNK), CHUNK)
        hot = (iotaf((n, CHUNK), 0) == where_row[0:1, at]).astype(F32)
        picked = lax.dot_general(
            ret_mat[...],
            hot,
            (((0,), (0,)), ((), ())),
            precision=lax.Precision.HIGHEST,
            preferred_element_type=F32,
        )
        spot = iotaf((span, CHUNK), 0) == where_row[1:2, at]
        best_out[:, at] = jnp.sum(jnp.where(spot, picked, 0.0), axis=0, keepdims=True)

    sent = send.at[pl.ds(part, n * part - part)]
    pltpu.make_async_copy(sent, sent, send_sem).wait()
    if over:
        sent = recv.at[pl.ds(0, n * over)]
        pltpu.make_async_copy(sent, sent, pass_send).wait()
    sent = lab_send.at[pl.ds(1, n - 1)]
    pltpu.make_async_copy(sent, sent, small_send.at[0]).wait()
    sent = ret_recv.at[pl.ds(1, n - 1)]
    pltpu.make_async_copy(sent, sent, small_send.at[1]).wait()


def exchange(embeddings, ids, slot_row, part, number):
    n_grp = lax.axis_size("grp")
    n_z = lax.axis_size("dev") // CORES
    n = n_grp * n_z * CORES
    rows, width = embeddings.shape
    clusters = slot_row.shape[1]
    owned = clusters // n
    quota = owned * MOST
    group = 4
    span = group * quota
    groups = n // group
    vmem = pl.BlockSpec(memory_space=pltpu.VMEM)
    return pl.pallas_call(
        functools.partial(kernel, n_grp, n_z, owned, quota, part, group),
        out_shape=(
            jax.ShapeDtypeStruct((1, rows), F32),
            jax.ShapeDtypeStruct((owned, width), F32),
            jax.ShapeDtypeStruct((1, 128), F32),
        ),
        in_specs=[pl.BlockSpec(memory_space=pl.ANY), vmem, vmem],
        out_specs=(vmem, vmem, vmem),
        scratch_shapes=[
            pltpu.VMEM((rows, width), BF16),
            pltpu.VMEM((n * part, width), BF16),
            pltpu.VMEM((n * quota, width), BF16),
            pltpu.VMEM((8, rows), F32),
            pltpu.VMEM((n, span + 128), F32),
            pltpu.VMEM((n, 1, span + 128), F32),
            pltpu.VMEM((n, 1, span + 128), F32),
            pltpu.VMEM((groups, 1, span), F32),
            pltpu.VMEM((groups, span, 1), F32),
            pltpu.VMEM((groups, 1, span), F32),
            pltpu.VMEM((n, 1, span), F32),
            pltpu.VMEM((n, span), F32),
            pltpu.VMEM((owned, width), F32),
            pltpu.SemaphoreType.DMA((rows // CHUNK,)),
            pltpu.SemaphoreType.DMA,
            pltpu.SemaphoreType.DMA((groups,)),
            pltpu.SemaphoreType.DMA,
            pltpu.SemaphoreType.DMA((groups,)),
            pltpu.SemaphoreType.DMA((2,)),
            pltpu.SemaphoreType.DMA((2,)),
        ],
        compiler_params=pltpu.CompilerParams(
            collective_id=number, has_side_effects=True, vmem_limit_bytes=60 * 1024 * 1024
        ),
    )(embeddings, ids, slot_row)


def local(embeddings, cluster_ids, cluster_slot):
    rows = embeddings.shape[0]
    clusters = cluster_slot.shape[0]
    ids = cluster_ids.reshape(1, rows)
    slot_row = cluster_slot.reshape(1, clusters)
    quota = clusters // lax.axis_size(("grp", "dev")) * MOST
    best, cent, crowded = exchange(embeddings, ids, slot_row, quota * 3 // 4, 0)

    def whole():
        again = exchange(embeddings, ids, slot_row, quota, 1)
        return again[0], again[1]

    best, cent = lax.cond(crowded[0, 0] > 0, whole, lambda: (best, cent))
    return best.reshape(rows), cent


def solution(mesh):
    in_specs = (P(("grp", "dev"), None), P(("grp", "dev"), None), P())
    out_specs = (P(("grp", "dev")), P(("grp", "dev"), None))
    return jax.shard_map(local, mesh=mesh, in_specs=in_specs, out_specs=out_specs, check_vma=False)
```

```python
import functools

import jax
import jax.numpy as jnp
from jax import lax
from jax.experimental import pallas as pl
from jax.experimental.pallas import tpu as pltpu
from jax.sharding import PartitionSpec as P

MOST = 8
CORES = 2
MESH = pl.DeviceIdType.MESH
F32 = jnp.float32
BF16 = jnp.bfloat16
CHUNK = 256


def iota(shape, dim):
    return lax.broadcasted_iota(jnp.int32, shape, dim)


def iotaf(shape, dim):
    return iota(shape, dim).astype(F32)


def floordiv(x, by):
    return jnp.floor((x + 0.5) * (1.0 / by))


def kernel(
    n_grp,
    n_z,
    owned,
    quota,
    part,
    group,
    emb,
    ids,
    slot_row,
    best_out,
    cent_out,
    flag_out,
    norm,
    send,
    recv,
    where_row,
    lab_mat,
    lab_send,
    lab_recv,
    lab_rows,
    lab_cols,
    best,
    ret_recv,
    ret_mat,
    sums,
    load_sem,
    send_sem,
    recv_sem,
    pass_send,
    pass_recv,
    small_send,
    small_recv,
):
    chips = n_grp * n_z
    n = chips * CORES
    pair = 2 * part
    over = quota - part
    rows = norm.shape[0]
    clusters = slot_row.shape[1]
    span = group * quota
    n_groups = n // group
    group_chips = group // CORES
    my_g = lax.axis_index("grp")
    my_d = lax.axis_index("dev")
    my_z = lax.div(my_d, CORES)
    my_c = lax.rem(my_d, CORES)

    def ahead(k):
        chip, core = lax.div(k, CORES), lax.rem(k, CORES)
        to_g = lax.rem(my_g + lax.div(chip, n_z), n_grp)
        return to_g, lax.rem(my_z + chip, n_z) * CORES + core

    def behind(k):
        chip, core = lax.div(k, CORES), lax.rem(k, CORES)
        to_g = lax.rem(my_g + n_grp - lax.div(chip, n_z), n_grp)
        return to_g, lax.rem(my_z + n_z - lax.rem(chip, n_z), n_z) * CORES + core

    barrier = pltpu.get_barrier_semaphore()

    @pl.loop(0, n, unroll=8)
    def _(k):
        @pl.when(k != my_c)
        def _():
            pl.semaphore_signal(barrier, inc=1, device_id=ahead(k), device_id_type=MESH)

    def load(c):
        at = pl.ds(pl.multiple_of(c * CHUNK, CHUNK), CHUNK)
        return pltpu.make_async_copy(emb.at[at], norm.at[at], load_sem.at[c])

    @pl.loop(0, rows // CHUNK)
    def _(c):
        load(c).start()

    eye = iota((clusters, clusters), 0) == iota((clusters, clusters), 1)
    slot_col = jnp.sum(jnp.where(eye, slot_row[...].astype(F32), 0.0), axis=1, keepdims=True)

    lab_mat[...] = jnp.zeros_like(lab_mat)
    before = (iota((CHUNK, CHUNK), 0) < iota((CHUNK, CHUNK), 1)).astype(BF16)
    grp_f = my_g.astype(F32)
    z_f = my_z.astype(F32)
    core_f = my_c.astype(F32)

    def place(c, carry):
        count, filled = carry
        at = pl.ds(pl.multiple_of(c * CHUNK, CHUNK), CHUNK)
        hit = iota((clusters, CHUNK), 0) == ids[:, at]
        slot = jnp.sum(jnp.where(hit, slot_col, 0.0), axis=0, keepdims=True)
        owner = floordiv(slot, owned)
        local = slot - owner * owned
        owner_chip = floordiv(owner, CORES)
        core = owner - owner_chip * CORES
        owner_grp = floordiv(owner_chip, n_z)
        kg = owner_grp - grp_f
        kz = owner_chip - owner_grp * n_z - z_f
        kg = jnp.where(kg < 0, kg + n_grp, kg)
        kz = jnp.where(kz < 0, kz + n_z, kz)
        chip = kg * n_z + kz
        k = chip * CORES + core
        hot = (iotaf((n, CHUNK), 0) == k).astype(F32)
        earlier = jnp.dot(hot.astype(BF16), before, preferred_element_type=F32) + count
        pos = jnp.sum(hot * earlier, axis=0, keepdims=True)
        line = jnp.where(core > 0, quota - 1 - pos, pos)
        in_group = chip - floordiv(chip, group_chips) * group_chips
        lane = (in_group * CORES + core_f) * quota + line
        where_row[0:1, at] = k
        where_row[1:2, at] = lane
        where_row[2:3, at] = chip * pair + core * (pair - quota) + line
        spot = (iotaf((span, CHUNK), 0) == lane).astype(BF16)
        lab_mat[:, 0:span] += lax.dot_general(
            (hot * (local + 1.0)).astype(BF16),
            spot,
            (((1,), (1,)), ((), ())),
            preferred_element_type=F32,
        )
        count = count + jnp.sum(hot, axis=1, keepdims=True)
        to_chip = (iotaf((chips, CHUNK), 0) == chip).astype(F32)
        return count, filled + jnp.sum(to_chip, axis=1, keepdims=True)

    _, filled = lax.fori_loop(
        0, rows // CHUNK, place, (jnp.zeros((n, 1), F32), jnp.zeros((chips, 1), F32))
    )
    crowded = jnp.max((filled > pair).astype(F32), axis=0, keepdims=True)
    lab_mat[:, span:] = jnp.broadcast_to(crowded, (n, lab_mat.shape[1] - span))

    @pl.loop(0, rows // CHUNK)
    def _(c):
        load(c).wait()
        at = pl.ds(pl.multiple_of(c * CHUNK, CHUNK), CHUNK)
        x = norm[at, :].astype(F32)
        norm[at, :] = (x * lax.rsqrt(jnp.sum(x * x, axis=1, keepdims=True) + 1e-06)).astype(BF16)

    made = group_chips * pair

    def make(g):
        spots = (iota((made, rows), 0) + g * made).astype(F32) == where_row[2:3, :]
        block = jnp.dot(spots.astype(BF16), norm[...], preferred_element_type=F32).astype(BF16)
        send[pl.ds(pl.multiple_of(g * made, made), made), :] = block

    def ship(g):
        @pl.loop(0, group, unroll=True)
        def _(j):
            k = g * group + j
            twin = lax.div(k, CORES) * CORES + my_c

            @pl.when(k != my_c)
            def _():
                to = twin * quota + lax.rem(k, CORES) * over
                pltpu.make_async_remote_copy(
                    src_ref=send.at[pl.ds(pl.multiple_of(k * part, 16), part)],
                    dst_ref=recv.at[pl.ds(pl.multiple_of(to, 16), part)],
                    send_sem=send_sem,
                    recv_sem=recv_sem.at[g],
                    device_id=ahead(k),
                    device_id_type=MESH,
                ).start()

    make(0)
    own = send[pl.ds(pl.multiple_of(my_c * part, 16), part), :]
    recv[pl.ds(pl.multiple_of(my_c * (quota + over), 16), part), :] = own
    lab_recv[my_c] = lab_mat[pl.ds(my_c, 1), :]

    @pl.loop(0, n, unroll=8)
    def _(k):
        lab_send[k] = lab_mat[pl.ds(k, 1), :]

    pl.semaphore_wait(barrier, n - 1)
    ship(0)

    @pl.loop(1, n_groups)
    def _(g):
        make(g)
        ship(g)

        @pl.when(g == 1)
        def _():
            @pl.loop(0, n, unroll=8)
            def _(k):
                @pl.when(k != my_c)
                def _():
                    pltpu.make_async_remote_copy(
                        src_ref=lab_send.at[k],
                        dst_ref=lab_recv.at[lax.div(k, CORES) * CORES + my_c],
                        send_sem=small_send.at[0],
                        recv_sem=small_recv.at[0],
                        device_id=ahead(k),
                        device_id_type=MESH,
                    ).start()

    others = lab_recv.at[pl.ds(1, n - 1)]
    pltpu.make_async_copy(others, others, small_recv.at[0]).wait()
    diag = iota((span, span), 0) == iota((span, span), 1)
    flag_out[...] = jnp.zeros_like(flag_out)

    @pl.loop(0, n_groups)
    def _(g):
        row = lab_recv[g * group]
        for j in range(1, group):
            row = row + lab_recv[g * group + j]
        lab_rows[g] = row[:, 0:span]
        lab_cols[g] = jnp.sum(jnp.where(diag, row[:, 0:span], 0.0), axis=1, keepdims=True)
        best[g] = jnp.full((1, span), -1.0, F32)
        flag_out[...] += row[:, span:]

    sums[...] = jnp.zeros_like(sums)

    def contract(a, b):
        return lax.dot_general(a, b, (((1,), (1,)), ((), ())), preferred_element_type=F32)

    def arrive(g):
        @pl.when(g == 0)
        def _():
            got = recv.at[pl.ds(0, (group - 1) * part)]
            pltpu.make_async_copy(got, got, recv_sem.at[0]).wait()

        @pl.when(g > 0)
        def _():
            got = recv.at[pl.ds(pl.multiple_of(g * span, span), group * part)]
            pltpu.make_async_copy(got, got, recv_sem.at[g]).wait()

        if over:
            @pl.loop(0, group, unroll=True)
            def _(j):
                base = (g * group + j) * quota
                start = base + (pair - quota) - my_c * (pair - quota - over)
                to = base + my_c * part
                pltpu.make_async_remote_copy(
                    src_ref=recv.at[pl.ds(pl.multiple_of(start, 16), over)],
                    dst_ref=recv.at[pl.ds(pl.multiple_of(to, 16), over)],
                    send_sem=pass_send,
                    recv_sem=pass_recv.at[g],
                    device_id=(my_g, my_z * CORES + (1 - my_c)),
                    device_id_type=MESH,
                ).start()

    def give(g):
        @pl.loop(0, group, unroll=True)
        def _(j):
            k = g * group + j

            @pl.when(k != my_c)
            def _():
                pltpu.make_async_remote_copy(
                    src_ref=best.at[g],
                    dst_ref=ret_recv.at[lax.div(k, CORES) * CORES + my_c],
                    send_sem=small_send.at[1],
                    recv_sem=small_recv.at[1],
                    device_id=behind(k),
                    device_id_type=MESH,
                ).start()

    def compare(g):
        if over:
            got = recv.at[pl.ds(pl.multiple_of(g * span, span), group * over)]
            pltpu.make_async_copy(got, got, pass_recv.at[g]).wait()
        new = recv[pl.ds(pl.multiple_of(g * span, span), span), :]
        member = iotaf((owned, span), 0) + 1.0 == lab_rows[g]
        sums[...] += jnp.dot(member.astype(BF16), new, preferred_element_type=F32)

        keep = (lab_cols[g] == lab_rows[g]) & ~diag
        top = jnp.max(jnp.where(keep, contract(new, new), -1.0), axis=0, keepdims=True)
        best[g] = jnp.maximum(best[g], top)

        @pl.loop(0, g)
        def _(h):
            old = recv[pl.ds(pl.multiple_of(h * span, span), span), :]
            keep = lab_cols[h] == lab_rows[g]
            top = jnp.max(jnp.where(keep, contract(old, new), -1.0), axis=0, keepdims=True)
            best[g] = jnp.maximum(best[g], top)
            keep = lab_cols[g] == lab_rows[h]
            top = jnp.max(jnp.where(keep, contract(new, old), -1.0), axis=0, keepdims=True)
            best[h] = jnp.maximum(best[h], top)

            @pl.when(g == n_groups - 1)
            def _():
                give(h)

        @pl.when(g == n_groups - 1)
        def _():
            give(g)

    @pl.loop(0, n_groups)
    def _(g):
        arrive(g)
        compare(g)

    ret_recv[my_c] = best[0]

    total = sums[...]
    cent_out[...] = total * lax.rsqrt(jnp.sum(total * total, axis=1, keepdims=True) + 1e-06)

    back = ret_recv.at[pl.ds(1, n - 1)]
    pltpu.make_async_copy(back, back, small_recv.at[1]).wait()

    @pl.loop(0, n, unroll=8)
    def _(k):
        ret_mat[pl.ds(k, 1), :] = ret_recv[k]

    @pl.loop(0, rows // CHUNK)
    def _(c):
        at = pl.ds(pl.multiple_of(c * CHUNK, CHUNK), CHUNK)
        hot = (iotaf((n, CHUNK), 0) == where_row[0:1, at]).astype(F32)
        picked = lax.dot_general(
            ret_mat[...],
            hot,
            (((0,), (0,)), ((), ())),
            precision=lax.Precision.HIGHEST,
            preferred_element_type=F32,
        )
        spot = iotaf((span, CHUNK), 0) == where_row[1:2, at]
        best_out[:, at] = jnp.sum(jnp.where(spot, picked, 0.0), axis=0, keepdims=True)

    sent = send.at[pl.ds(part, n * part - part)]
    pltpu.make_async_copy(sent, sent, send_sem).wait()
    if over:
        sent = recv.at[pl.ds(0, n * over)]
        pltpu.make_async_copy(sent, sent, pass_send).wait()
    sent = lab_send.at[pl.ds(1, n - 1)]
    pltpu.make_async_copy(sent, sent, small_send.at[0]).wait()
    sent = ret_recv.at[pl.ds(1, n - 1)]
    pltpu.make_async_copy(sent, sent, small_send.at[1]).wait()


def exchange(embeddings, ids, slot_row, part, number):
    n_grp = lax.axis_size("grp")
    n_z = lax.axis_size("dev") // CORES
    n = n_grp * n_z * CORES
    rows, width = embeddings.shape
    clusters = slot_row.shape[1]
    owned = clusters // n
    quota = owned * MOST
    group = 4
    span = group * quota
    groups = n // group
    vmem = pl.BlockSpec(memory_space=pltpu.VMEM)
    return pl.pallas_call(
        functools.partial(kernel, n_grp, n_z, owned, quota, part, group),
        out_shape=(
            jax.ShapeDtypeStruct((1, rows), F32),
            jax.ShapeDtypeStruct((owned, width), F32),
            jax.ShapeDtypeStruct((1, 128), F32),
        ),
        in_specs=[pl.BlockSpec(memory_space=pl.ANY), vmem, vmem],
        out_specs=(vmem, vmem, vmem),
        scratch_shapes=[
            pltpu.VMEM((rows, width), BF16),
            pltpu.VMEM((n * part, width), BF16),
            pltpu.VMEM((n * quota, width), BF16),
            pltpu.VMEM((8, rows), F32),
            pltpu.VMEM((n, span + 128), F32),
            pltpu.VMEM((n, 1, span + 128), F32),
            pltpu.VMEM((n, 1, span + 128), F32),
            pltpu.VMEM((groups, 1, span), F32),
            pltpu.VMEM((groups, span, 1), F32),
            pltpu.VMEM((groups, 1, span), F32),
            pltpu.VMEM((n, 1, span), F32),
            pltpu.VMEM((n, span), F32),
            pltpu.VMEM((owned, width), F32),
            pltpu.SemaphoreType.DMA((rows // CHUNK,)),
            pltpu.SemaphoreType.DMA,
            pltpu.SemaphoreType.DMA((groups,)),
            pltpu.SemaphoreType.DMA,
            pltpu.SemaphoreType.DMA((groups,)),
            pltpu.SemaphoreType.DMA((2,)),
            pltpu.SemaphoreType.DMA((2,)),
        ],
        compiler_params=pltpu.CompilerParams(
            collective_id=number, has_side_effects=True, vmem_limit_bytes=60 * 1024 * 1024
        ),
    )(embeddings, ids, slot_row)


def local(embeddings, cluster_ids, cluster_slot):
    rows = embeddings.shape[0]
    clusters = cluster_slot.shape[0]
    ids = cluster_ids.reshape(1, rows)
    slot_row = cluster_slot.reshape(1, clusters)
    quota = clusters // lax.axis_size(("grp", "dev")) * MOST
    best, cent, crowded = exchange(embeddings, ids, slot_row, quota * 3 // 4, 0)

    def whole():
        again = exchange(embeddings, ids, slot_row, quota, 1)
        return again[0], again[1]

    best, cent = lax.cond(crowded[0, 0] > 0, whole, lambda: (best, cent))
    return best.reshape(rows), cent


def solution(mesh):
    in_specs = (P(("grp", "dev"), None), P(("grp", "dev"), None), P())
    out_specs = (P(("grp", "dev")), P(("grp", "dev"), None))
    return jax.shard_map(local, mesh=mesh, in_specs=in_specs, out_specs=out_specs, check_vma=False)
```

```python
import functools

import jax
import jax.numpy as jnp
from jax import lax
from jax.experimental import pallas as pl
from jax.experimental.pallas import tpu as pltpu
from jax.sharding import PartitionSpec as P

MOST = 8
CORES = 2
MESH = pl.DeviceIdType.MESH
F32 = jnp.float32
BF16 = jnp.bfloat16
CHUNK = 256


def iota(shape, dim):
    return lax.broadcasted_iota(jnp.int32, shape, dim)


def iotaf(shape, dim):
    return iota(shape, dim).astype(F32)


def floordiv(x, by):
    return jnp.floor((x + 0.5) * (1.0 / by))


def kernel(
    n_grp,
    n_z,
    owned,
    quota,
    part,
    group,
    emb,
    ids,
    slot_row,
    best_out,
    cent_out,
    flag_out,
    norm,
    send,
    recv,
    where_row,
    lab_mat,
    lab_send,
    lab_recv,
    lab_rows,
    lab_cols,
    best,
    ret_recv,
    ret_mat,
    sums,
    load_sem,
    send_sem,
    recv_sem,
    pass_send,
    pass_recv,
    small_send,
    small_recv,
):
    chips = n_grp * n_z
    n = chips * CORES
    pair = 2 * part
    over = quota - part
    rows = norm.shape[0]
    clusters = slot_row.shape[1]
    span = group * quota
    n_groups = n // group
    group_chips = group // CORES
    my_g = lax.axis_index("grp")
    my_d = lax.axis_index("dev")
    my_z = lax.div(my_d, CORES)
    my_c = lax.rem(my_d, CORES)

    def ahead(k):
        chip, core = lax.div(k, CORES), lax.rem(k, CORES)
        to_g = lax.rem(my_g + lax.div(chip, n_z), n_grp)
        return to_g, lax.rem(my_z + chip, n_z) * CORES + core

    def behind(k):
        chip, core = lax.div(k, CORES), lax.rem(k, CORES)
        to_g = lax.rem(my_g + n_grp - lax.div(chip, n_z), n_grp)
        return to_g, lax.rem(my_z + n_z - lax.rem(chip, n_z), n_z) * CORES + core

    barrier = pltpu.get_barrier_semaphore()

    @pl.loop(0, n, unroll=8)
    def _(k):
        @pl.when(k != my_c)
        def _():
            pl.semaphore_signal(barrier, inc=1, device_id=ahead(k), device_id_type=MESH)

    def load(c):
        at = pl.ds(pl.multiple_of(c * CHUNK, CHUNK), CHUNK)
        return pltpu.make_async_copy(emb.at[at], norm.at[at], load_sem.at[c])

    @pl.loop(0, rows // CHUNK)
    def _(c):
        load(c).start()

    eye = iota((clusters, clusters), 0) == iota((clusters, clusters), 1)
    slot_col = jnp.sum(jnp.where(eye, slot_row[...].astype(F32), 0.0), axis=1, keepdims=True)

    lab_mat[...] = jnp.zeros_like(lab_mat)
    before = (iota((CHUNK, CHUNK), 0) < iota((CHUNK, CHUNK), 1)).astype(BF16)
    grp_f = my_g.astype(F32)
    z_f = my_z.astype(F32)
    core_f = my_c.astype(F32)

    def place(c, carry):
        count, filled = carry
        at = pl.ds(pl.multiple_of(c * CHUNK, CHUNK), CHUNK)
        hit = iota((clusters, CHUNK), 0) == ids[:, at]
        slot = jnp.sum(jnp.where(hit, slot_col, 0.0), axis=0, keepdims=True)
        owner = floordiv(slot, owned)
        local = slot - owner * owned
        owner_chip = floordiv(owner, CORES)
        core = owner - owner_chip * CORES
        owner_grp = floordiv(owner_chip, n_z)
        kg = owner_grp - grp_f
        kz = owner_chip - owner_grp * n_z - z_f
        kg = jnp.where(kg < 0, kg + n_grp, kg)
        kz = jnp.where(kz < 0, kz + n_z, kz)
        chip = kg * n_z + kz
        k = chip * CORES + core
        hot = (iotaf((n, CHUNK), 0) == k).astype(F32)
        earlier = jnp.dot(hot.astype(BF16), before, preferred_element_type=F32) + count
        pos = jnp.sum(hot * earlier, axis=0, keepdims=True)
        line = jnp.where(core > 0, quota - 1 - pos, pos)
        in_group = chip - floordiv(chip, group_chips) * group_chips
        lane = (in_group * CORES + core_f) * quota + line
        where_row[0:1, at] = k
        where_row[1:2, at] = lane
        where_row[2:3, at] = chip * pair + core * (pair - quota) + line
        spot = (iotaf((span, CHUNK), 0) == lane).astype(BF16)
        lab_mat[:, 0:span] += lax.dot_general(
            (hot * (local + 1.0)).astype(BF16),
            spot,
            (((1,), (1,)), ((), ())),
            preferred_element_type=F32,
        )
        count = count + jnp.sum(hot, axis=1, keepdims=True)
        to_chip = (iotaf((chips, CHUNK), 0) == chip).astype(F32)
        return count, filled + jnp.sum(to_chip, axis=1, keepdims=True)

    _, filled = lax.fori_loop(
        0, rows // CHUNK, place, (jnp.zeros((n, 1), F32), jnp.zeros((chips, 1), F32))
    )
    crowded = jnp.max((filled > pair).astype(F32), axis=0, keepdims=True)
    lab_mat[:, span:] = jnp.broadcast_to(crowded, (n, lab_mat.shape[1] - span))

    @pl.loop(0, rows // CHUNK)
    def _(c):
        load(c).wait()
        at = pl.ds(pl.multiple_of(c * CHUNK, CHUNK), CHUNK)
        x = norm[at, :].astype(F32)
        norm[at, :] = (x * lax.rsqrt(jnp.sum(x * x, axis=1, keepdims=True) + 1e-06)).astype(BF16)

    made = group_chips * pair

    def make(g):
        spots = (iota((made, rows), 0) + g * made).astype(F32) == where_row[2:3, :]
        block = jnp.dot(spots.astype(BF16), norm[...], preferred_element_type=F32).astype(BF16)
        send[pl.ds(pl.multiple_of(g * made, made), made), :] = block

    def ship(g):
        @pl.loop(0, group, unroll=True)
        def _(j):
            k = g * group + j
            twin = lax.div(k, CORES) * CORES + my_c

            @pl.when(k != my_c)
            def _():
                to = twin * quota + lax.rem(k, CORES) * over
                pltpu.make_async_remote_copy(
                    src_ref=send.at[pl.ds(pl.multiple_of(k * part, 16), part)],
                    dst_ref=recv.at[pl.ds(pl.multiple_of(to, 16), part)],
                    send_sem=send_sem,
                    recv_sem=recv_sem.at[g],
                    device_id=ahead(k),
                    device_id_type=MESH,
                ).start()

    make(0)
    own = send[pl.ds(pl.multiple_of(my_c * part, 16), part), :]
    recv[pl.ds(pl.multiple_of(my_c * (quota + over), 16), part), :] = own
    lab_recv[my_c] = lab_mat[pl.ds(my_c, 1), :]

    @pl.loop(0, n, unroll=8)
    def _(k):
        lab_send[k] = lab_mat[pl.ds(k, 1), :]

    pl.semaphore_wait(barrier, n - 1)
    @pl.loop(0, n, unroll=8)
    def _(k):
        @pl.when(k != my_c)
        def _():
            pltpu.make_async_remote_copy(
                src_ref=lab_send.at[k],
                dst_ref=lab_recv.at[lax.div(k, CORES) * CORES + my_c],
                send_sem=small_send.at[0],
                recv_sem=small_recv.at[0],
                device_id=ahead(k),
                device_id_type=MESH,
            ).start()

    ship(0)

    @pl.loop(1, n_groups)
    def _(g):
        make(g)
        ship(g)

    others = lab_recv.at[pl.ds(1, n - 1)]
    pltpu.make_async_copy(others, others, small_recv.at[0]).wait()
    diag = iota((span, span), 0) == iota((span, span), 1)
    flag_out[...] = jnp.zeros_like(flag_out)

    @pl.loop(0, n_groups)
    def _(g):
        row = lab_recv[g * group]
        for j in range(1, group):
            row = row + lab_recv[g * group + j]
        lab_rows[g] = row[:, 0:span]
        lab_cols[g] = jnp.sum(jnp.where(diag, row[:, 0:span], 0.0), axis=1, keepdims=True)
        best[g] = jnp.full((1, span), -1.0, F32)
        flag_out[...] += row[:, span:]

    sums[...] = jnp.zeros_like(sums)

    def contract(a, b):
        return lax.dot_general(a, b, (((1,), (1,)), ((), ())), preferred_element_type=F32)

    def arrive(g):
        @pl.when(g == 0)
        def _():
            got = recv.at[pl.ds(0, (group - 1) * part)]
            pltpu.make_async_copy(got, got, recv_sem.at[0]).wait()

        @pl.when(g > 0)
        def _():
            got = recv.at[pl.ds(pl.multiple_of(g * span, span), group * part)]
            pltpu.make_async_copy(got, got, recv_sem.at[g]).wait()

        if over:
            @pl.loop(0, group, unroll=True)
            def _(j):
                base = (g * group + j) * quota
                start = base + (pair - quota) - my_c * (pair - quota - over)
                to = base + my_c * part
                pltpu.make_async_remote_copy(
                    src_ref=recv.at[pl.ds(pl.multiple_of(start, 16), over)],
                    dst_ref=recv.at[pl.ds(pl.multiple_of(to, 16), over)],
                    send_sem=pass_send,
                    recv_sem=pass_recv.at[g],
                    device_id=(my_g, my_z * CORES + (1 - my_c)),
                    device_id_type=MESH,
                ).start()

    def give(g):
        @pl.loop(0, group, unroll=True)
        def _(j):
            k = g * group + j

            @pl.when(k != my_c)
            def _():
                pltpu.make_async_remote_copy(
                    src_ref=best.at[g],
                    dst_ref=ret_recv.at[lax.div(k, CORES) * CORES + my_c],
                    send_sem=small_send.at[1],
                    recv_sem=small_recv.at[1],
                    device_id=behind(k),
                    device_id_type=MESH,
                ).start()

    def compare(g):
        if over:
            got = recv.at[pl.ds(pl.multiple_of(g * span, span), group * over)]
            pltpu.make_async_copy(got, got, pass_recv.at[g]).wait()
        new = recv[pl.ds(pl.multiple_of(g * span, span), span), :]
        member = iotaf((owned, span), 0) + 1.0 == lab_rows[g]
        sums[...] += jnp.dot(member.astype(BF16), new, preferred_element_type=F32)

        keep = (lab_cols[g] == lab_rows[g]) & ~diag
        top = jnp.max(jnp.where(keep, contract(new, new), -1.0), axis=0, keepdims=True)
        best[g] = jnp.maximum(best[g], top)

        @pl.loop(0, g)
        def _(h):
            old = recv[pl.ds(pl.multiple_of(h * span, span), span), :]
            keep = lab_cols[h] == lab_rows[g]
            top = jnp.max(jnp.where(keep, contract(old, new), -1.0), axis=0, keepdims=True)
            best[g] = jnp.maximum(best[g], top)
            keep = lab_cols[g] == lab_rows[h]
            top = jnp.max(jnp.where(keep, contract(new, old), -1.0), axis=0, keepdims=True)
            best[h] = jnp.maximum(best[h], top)

            @pl.when(g == n_groups - 1)
            def _():
                give(h)

        @pl.when(g == n_groups - 1)
        def _():
            give(g)

    @pl.loop(0, n_groups)
    def _(g):
        arrive(g)
        compare(g)

    ret_recv[my_c] = best[0]

    total = sums[...]
    cent_out[...] = total * lax.rsqrt(jnp.sum(total * total, axis=1, keepdims=True) + 1e-06)

    back = ret_recv.at[pl.ds(1, n - 1)]
    pltpu.make_async_copy(back, back, small_recv.at[1]).wait()

    @pl.loop(0, n, unroll=8)
    def _(k):
        ret_mat[pl.ds(k, 1), :] = ret_recv[k]

    @pl.loop(0, rows // CHUNK)
    def _(c):
        at = pl.ds(pl.multiple_of(c * CHUNK, CHUNK), CHUNK)
        hot = (iotaf((n, CHUNK), 0) == where_row[0:1, at]).astype(F32)
        picked = lax.dot_general(
            ret_mat[...],
            hot,
            (((0,), (0,)), ((), ())),
            precision=lax.Precision.HIGHEST,
            preferred_element_type=F32,
        )
        spot = iotaf((span, CHUNK), 0) == where_row[1:2, at]
        best_out[:, at] = jnp.sum(jnp.where(spot, picked, 0.0), axis=0, keepdims=True)

    sent = send.at[pl.ds(part, n * part - part)]
    pltpu.make_async_copy(sent, sent, send_sem).wait()
    if over:
        sent = recv.at[pl.ds(0, n * over)]
        pltpu.make_async_copy(sent, sent, pass_send).wait()
    sent = lab_send.at[pl.ds(1, n - 1)]
    pltpu.make_async_copy(sent, sent, small_send.at[0]).wait()
    sent = ret_recv.at[pl.ds(1, n - 1)]
    pltpu.make_async_copy(sent, sent, small_send.at[1]).wait()


def exchange(embeddings, ids, slot_row, part, number):
    n_grp = lax.axis_size("grp")
    n_z = lax.axis_size("dev") // CORES
    n = n_grp * n_z * CORES
    rows, width = embeddings.shape
    clusters = slot_row.shape[1]
    owned = clusters // n
    quota = owned * MOST
    group = 4
    span = group * quota
    groups = n // group
    vmem = pl.BlockSpec(memory_space=pltpu.VMEM)
    return pl.pallas_call(
        functools.partial(kernel, n_grp, n_z, owned, quota, part, group),
        out_shape=(
            jax.ShapeDtypeStruct((1, rows), F32),
            jax.ShapeDtypeStruct((owned, width), F32),
            jax.ShapeDtypeStruct((1, 128), F32),
        ),
        in_specs=[pl.BlockSpec(memory_space=pl.ANY), vmem, vmem],
        out_specs=(vmem, vmem, vmem),
        scratch_shapes=[
            pltpu.VMEM((rows, width), BF16),
            pltpu.VMEM((n * part, width), BF16),
            pltpu.VMEM((n * quota, width), BF16),
            pltpu.VMEM((8, rows), F32),
            pltpu.VMEM((n, span + 128), F32),
            pltpu.VMEM((n, 1, span + 128), F32),
            pltpu.VMEM((n, 1, span + 128), F32),
            pltpu.VMEM((groups, 1, span), F32),
            pltpu.VMEM((groups, span, 1), F32),
            pltpu.VMEM((groups, 1, span), F32),
            pltpu.VMEM((n, 1, span), F32),
            pltpu.VMEM((n, span), F32),
            pltpu.VMEM((owned, width), F32),
            pltpu.SemaphoreType.DMA((rows // CHUNK,)),
            pltpu.SemaphoreType.DMA,
            pltpu.SemaphoreType.DMA((groups,)),
            pltpu.SemaphoreType.DMA,
            pltpu.SemaphoreType.DMA((groups,)),
            pltpu.SemaphoreType.DMA((2,)),
            pltpu.SemaphoreType.DMA((2,)),
        ],
        compiler_params=pltpu.CompilerParams(
            collective_id=number, has_side_effects=True, vmem_limit_bytes=60 * 1024 * 1024
        ),
    )(embeddings, ids, slot_row)


def local(embeddings, cluster_ids, cluster_slot):
    rows = embeddings.shape[0]
    clusters = cluster_slot.shape[0]
    ids = cluster_ids.reshape(1, rows)
    slot_row = cluster_slot.reshape(1, clusters)
    quota = clusters // lax.axis_size(("grp", "dev")) * MOST
    best, cent, crowded = exchange(embeddings, ids, slot_row, quota * 3 // 4, 0)

    def whole():
        again = exchange(embeddings, ids, slot_row, quota, 1)
        return again[0], again[1]

    best, cent = lax.cond(crowded[0, 0] > 0, whole, lambda: (best, cent))
    return best.reshape(rows), cent


def solution(mesh):
    in_specs = (P(("grp", "dev"), None), P(("grp", "dev"), None), P())
    out_specs = (P(("grp", "dev")), P(("grp", "dev"), None))
    return jax.shard_map(local, mesh=mesh, in_specs=in_specs, out_specs=out_specs, check_vma=False)
```

```python
import functools

import jax
import jax.numpy as jnp
from jax import lax
from jax.experimental import pallas as pl
from jax.experimental.pallas import tpu as pltpu
from jax.sharding import PartitionSpec as P

MOST = 8
CORES = 2
MESH = pl.DeviceIdType.MESH
F32 = jnp.float32
BF16 = jnp.bfloat16
CHUNK = 256


def iota(shape, dim):
    return lax.broadcasted_iota(jnp.int32, shape, dim)


def iotaf(shape, dim):
    return iota(shape, dim).astype(F32)


def floordiv(x, by):
    return jnp.floor((x + 0.5) * (1.0 / by))


def kernel(
    n_grp,
    n_z,
    owned,
    quota,
    part,
    group,
    emb,
    ids,
    slot_row,
    best_out,
    cent_out,
    flag_out,
    norm,
    send,
    recv,
    where_row,
    lab_mat,
    lab_send,
    lab_recv,
    lab_rows,
    lab_cols,
    best,
    ret_recv,
    ret_mat,
    sums,
    load_sem,
    send_sem,
    recv_sem,
    pass_send,
    pass_recv,
    small_send,
    small_recv,
):
    chips = n_grp * n_z
    n = chips * CORES
    pair = 2 * part
    over = quota - part
    rows = norm.shape[0]
    clusters = slot_row.shape[1]
    span = group * quota
    n_groups = n // group
    group_chips = group // CORES
    my_g = lax.axis_index("grp")
    my_d = lax.axis_index("dev")
    my_z = lax.div(my_d, CORES)
    my_c = lax.rem(my_d, CORES)

    def ahead(k):
        chip, core = lax.div(k, CORES), lax.rem(k, CORES)
        to_g = lax.rem(my_g + lax.div(chip, n_z) + lax.rem(chip, n_z), n_grp)
        return to_g, lax.rem(my_z + chip, n_z) * CORES + core

    def behind(k):
        chip, core = lax.div(k, CORES), lax.rem(k, CORES)
        back = lax.rem(lax.div(chip, n_z) + lax.rem(chip, n_z), n_grp)
        to_g = lax.rem(my_g + n_grp - back, n_grp)
        return to_g, lax.rem(my_z + n_z - lax.rem(chip, n_z), n_z) * CORES + core

    barrier = pltpu.get_barrier_semaphore()

    @pl.loop(0, n, unroll=8)
    def _(k):
        @pl.when(k != my_c)
        def _():
            pl.semaphore_signal(barrier, inc=1, device_id=ahead(k), device_id_type=MESH)

    def load(c):
        at = pl.ds(pl.multiple_of(c * CHUNK, CHUNK), CHUNK)
        return pltpu.make_async_copy(emb.at[at], norm.at[at], load_sem.at[c])

    @pl.loop(0, rows // CHUNK)
    def _(c):
        load(c).start()

    eye = iota((clusters, clusters), 0) == iota((clusters, clusters), 1)
    slot_col = jnp.sum(jnp.where(eye, slot_row[...].astype(F32), 0.0), axis=1, keepdims=True)

    lab_mat[...] = jnp.zeros_like(lab_mat)
    before = (iota((CHUNK, CHUNK), 0) < iota((CHUNK, CHUNK), 1)).astype(BF16)
    grp_f = my_g.astype(F32)
    z_f = my_z.astype(F32)
    core_f = my_c.astype(F32)

    def place(c, carry):
        count, filled = carry
        at = pl.ds(pl.multiple_of(c * CHUNK, CHUNK), CHUNK)
        hit = iota((clusters, CHUNK), 0) == ids[:, at]
        slot = jnp.sum(jnp.where(hit, slot_col, 0.0), axis=0, keepdims=True)
        owner = floordiv(slot, owned)
        local = slot - owner * owned
        owner_chip = floordiv(owner, CORES)
        core = owner - owner_chip * CORES
        owner_grp = floordiv(owner_chip, n_z)
        kg = owner_grp - grp_f
        kz = owner_chip - owner_grp * n_z - z_f
        kg = jnp.where(kg < 0, kg + n_grp, kg)
        kz = jnp.where(kz < 0, kz + n_z, kz)
        turn = kg + n_z * n_grp - kz
        chip = (turn - floordiv(turn, n_grp) * n_grp) * n_z + kz
        k = chip * CORES + core
        hot = (iotaf((n, CHUNK), 0) == k).astype(F32)
        earlier = jnp.dot(hot.astype(BF16), before, preferred_element_type=F32) + count
        pos = jnp.sum(hot * earlier, axis=0, keepdims=True)
        line = jnp.where(core > 0, quota - 1 - pos, pos)
        in_group = chip - floordiv(chip, group_chips) * group_chips
        lane = (in_group * CORES + core_f) * quota + line
        where_row[0:1, at] = k
        where_row[1:2, at] = lane
        where_row[2:3, at] = chip * pair + core * (pair - quota) + line
        spot = (iotaf((span, CHUNK), 0) == lane).astype(BF16)
        lab_mat[:, 0:span] += lax.dot_general(
            (hot * (local + 1.0)).astype(BF16),
            spot,
            (((1,), (1,)), ((), ())),
            preferred_element_type=F32,
        )
        count = count + jnp.sum(hot, axis=1, keepdims=True)
        to_chip = (iotaf((chips, CHUNK), 0) == chip).astype(F32)
        return count, filled + jnp.sum(to_chip, axis=1, keepdims=True)

    _, filled = lax.fori_loop(
        0, rows // CHUNK, place, (jnp.zeros((n, 1), F32), jnp.zeros((chips, 1), F32))
    )
    crowded = jnp.max((filled > pair).astype(F32), axis=0, keepdims=True)
    lab_mat[:, span:] = jnp.broadcast_to(crowded, (n, lab_mat.shape[1] - span))

    @pl.loop(0, rows // CHUNK)
    def _(c):
        load(c).wait()
        at = pl.ds(pl.multiple_of(c * CHUNK, CHUNK), CHUNK)
        x = norm[at, :].astype(F32)
        norm[at, :] = (x * lax.rsqrt(jnp.sum(x * x, axis=1, keepdims=True) + 1e-06)).astype(BF16)

    made = group_chips * pair

    def make(g):
        spots = (iota((made, rows), 0) + g * made).astype(F32) == where_row[2:3, :]
        block = jnp.dot(spots.astype(BF16), norm[...], preferred_element_type=F32).astype(BF16)
        send[pl.ds(pl.multiple_of(g * made, made), made), :] = block

    def ship(g):
        @pl.loop(0, group, unroll=True)
        def _(j):
            k = g * group + j
            twin = lax.div(k, CORES) * CORES + my_c

            @pl.when(k != my_c)
            def _():
                to = twin * quota + lax.rem(k, CORES) * over
                pltpu.make_async_remote_copy(
                    src_ref=send.at[pl.ds(pl.multiple_of(k * part, 16), part)],
                    dst_ref=recv.at[pl.ds(pl.multiple_of(to, 16), part)],
                    send_sem=send_sem,
                    recv_sem=recv_sem.at[g],
                    device_id=ahead(k),
                    device_id_type=MESH,
                ).start()

    make(0)
    own = send[pl.ds(pl.multiple_of(my_c * part, 16), part), :]
    recv[pl.ds(pl.multiple_of(my_c * (quota + over), 16), part), :] = own
    lab_recv[my_c] = lab_mat[pl.ds(my_c, 1), :]

    @pl.loop(0, n, unroll=8)
    def _(k):
        lab_send[k] = lab_mat[pl.ds(k, 1), :]

    pl.semaphore_wait(barrier, n - 1)
    @pl.loop(0, n, unroll=8)
    def _(k):
        @pl.when(k != my_c)
        def _():
            pltpu.make_async_remote_copy(
                src_ref=lab_send.at[k],
                dst_ref=lab_recv.at[lax.div(k, CORES) * CORES + my_c],
                send_sem=small_send.at[0],
                recv_sem=small_recv.at[0],
                device_id=ahead(k),
                device_id_type=MESH,
            ).start()

    ship(0)

    @pl.loop(1, n_groups)
    def _(g):
        make(g)
        ship(g)

    others = lab_recv.at[pl.ds(1, n - 1)]
    pltpu.make_async_copy(others, others, small_recv.at[0]).wait()
    diag = iota((span, span), 0) == iota((span, span), 1)
    flag_out[...] = jnp.zeros_like(flag_out)

    @pl.loop(0, n_groups)
    def _(g):
        row = lab_recv[g * group]
        for j in range(1, group):
            row = row + lab_recv[g * group + j]
        lab_rows[g] = row[:, 0:span]
        lab_cols[g] = jnp.sum(jnp.where(diag, row[:, 0:span], 0.0), axis=1, keepdims=True)
        best[g] = jnp.full((1, span), -1.0, F32)
        flag_out[...] += row[:, span:]

    sums[...] = jnp.zeros_like(sums)

    def contract(a, b):
        return lax.dot_general(a, b, (((1,), (1,)), ((), ())), preferred_element_type=F32)

    def arrive(g):
        @pl.when(g == 0)
        def _():
            got = recv.at[pl.ds(0, (group - 1) * part)]
            pltpu.make_async_copy(got, got, recv_sem.at[0]).wait()

        @pl.when(g > 0)
        def _():
            got = recv.at[pl.ds(pl.multiple_of(g * span, span), group * part)]
            pltpu.make_async_copy(got, got, recv_sem.at[g]).wait()

        if over:
            @pl.loop(0, group, unroll=True)
            def _(j):
                base = (g * group + j) * quota
                start = base + (pair - quota) - my_c * (pair - quota - over)
                to = base + my_c * part
                pltpu.make_async_remote_copy(
                    src_ref=recv.at[pl.ds(pl.multiple_of(start, 16), over)],
                    dst_ref=recv.at[pl.ds(pl.multiple_of(to, 16), over)],
                    send_sem=pass_send,
                    recv_sem=pass_recv.at[g],
                    device_id=(my_g, my_z * CORES + (1 - my_c)),
                    device_id_type=MESH,
                ).start()

    def give(g):
        @pl.loop(0, group, unroll=True)
        def _(j):
            k = g * group + j

            @pl.when(k != my_c)
            def _():
                pltpu.make_async_remote_copy(
                    src_ref=best.at[g],
                    dst_ref=ret_recv.at[lax.div(k, CORES) * CORES + my_c],
                    send_sem=small_send.at[1],
                    recv_sem=small_recv.at[1],
                    device_id=behind(k),
                    device_id_type=MESH,
                ).start()

    def compare(g):
        if over:
            got = recv.at[pl.ds(pl.multiple_of(g * span, span), group * over)]
            pltpu.make_async_copy(got, got, pass_recv.at[g]).wait()
        new = recv[pl.ds(pl.multiple_of(g * span, span), span), :]
        member = iotaf((owned, span), 0) + 1.0 == lab_rows[g]
        sums[...] += jnp.dot(member.astype(BF16), new, preferred_element_type=F32)

        keep = (lab_cols[g] == lab_rows[g]) & ~diag
        top = jnp.max(jnp.where(keep, contract(new, new), -1.0), axis=0, keepdims=True)
        best[g] = jnp.maximum(best[g], top)

        @pl.loop(0, g)
        def _(h):
            old = recv[pl.ds(pl.multiple_of(h * span, span), span), :]
            keep = lab_cols[h] == lab_rows[g]
            top = jnp.max(jnp.where(keep, contract(old, new), -1.0), axis=0, keepdims=True)
            best[g] = jnp.maximum(best[g], top)
            keep = lab_cols[g] == lab_rows[h]
            top = jnp.max(jnp.where(keep, contract(new, old), -1.0), axis=0, keepdims=True)
            best[h] = jnp.maximum(best[h], top)

            @pl.when(g == n_groups - 1)
            def _():
                give(h)

        @pl.when(g == n_groups - 1)
        def _():
            give(g)

    @pl.loop(0, n_groups)
    def _(g):
        arrive(g)
        compare(g)

    ret_recv[my_c] = best[0]

    total = sums[...]
    cent_out[...] = total * lax.rsqrt(jnp.sum(total * total, axis=1, keepdims=True) + 1e-06)

    back = ret_recv.at[pl.ds(1, n - 1)]
    pltpu.make_async_copy(back, back, small_recv.at[1]).wait()

    @pl.loop(0, n, unroll=8)
    def _(k):
        ret_mat[pl.ds(k, 1), :] = ret_recv[k]

    @pl.loop(0, rows // CHUNK)
    def _(c):
        at = pl.ds(pl.multiple_of(c * CHUNK, CHUNK), CHUNK)
        hot = (iotaf((n, CHUNK), 0) == where_row[0:1, at]).astype(F32)
        picked = lax.dot_general(
            ret_mat[...],
            hot,
            (((0,), (0,)), ((), ())),
            precision=lax.Precision.HIGHEST,
            preferred_element_type=F32,
        )
        spot = iotaf((span, CHUNK), 0) == where_row[1:2, at]
        best_out[:, at] = jnp.sum(jnp.where(spot, picked, 0.0), axis=0, keepdims=True)

    sent = send.at[pl.ds(part, n * part - part)]
    pltpu.make_async_copy(sent, sent, send_sem).wait()
    if over:
        sent = recv.at[pl.ds(0, n * over)]
        pltpu.make_async_copy(sent, sent, pass_send).wait()
    sent = lab_send.at[pl.ds(1, n - 1)]
    pltpu.make_async_copy(sent, sent, small_send.at[0]).wait()
    sent = ret_recv.at[pl.ds(1, n - 1)]
    pltpu.make_async_copy(sent, sent, small_send.at[1]).wait()


def exchange(embeddings, ids, slot_row, part, number):
    n_grp = lax.axis_size("grp")
    n_z = lax.axis_size("dev") // CORES
    n = n_grp * n_z * CORES
    rows, width = embeddings.shape
    clusters = slot_row.shape[1]
    owned = clusters // n
    quota = owned * MOST
    group = 4
    span = group * quota
    groups = n // group
    vmem = pl.BlockSpec(memory_space=pltpu.VMEM)
    return pl.pallas_call(
        functools.partial(kernel, n_grp, n_z, owned, quota, part, group),
        out_shape=(
            jax.ShapeDtypeStruct((1, rows), F32),
            jax.ShapeDtypeStruct((owned, width), F32),
            jax.ShapeDtypeStruct((1, 128), F32),
        ),
        in_specs=[pl.BlockSpec(memory_space=pl.ANY), vmem, vmem],
        out_specs=(vmem, vmem, vmem),
        scratch_shapes=[
            pltpu.VMEM((rows, width), BF16),
            pltpu.VMEM((n * part, width), BF16),
            pltpu.VMEM((n * quota, width), BF16),
            pltpu.VMEM((8, rows), F32),
            pltpu.VMEM((n, span + 128), F32),
            pltpu.VMEM((n, 1, span + 128), F32),
            pltpu.VMEM((n, 1, span + 128), F32),
            pltpu.VMEM((groups, 1, span), F32),
            pltpu.VMEM((groups, span, 1), F32),
            pltpu.VMEM((groups, 1, span), F32),
            pltpu.VMEM((n, 1, span), F32),
            pltpu.VMEM((n, span), F32),
            pltpu.VMEM((owned, width), F32),
            pltpu.SemaphoreType.DMA((rows // CHUNK,)),
            pltpu.SemaphoreType.DMA,
            pltpu.SemaphoreType.DMA((groups,)),
            pltpu.SemaphoreType.DMA,
            pltpu.SemaphoreType.DMA((groups,)),
            pltpu.SemaphoreType.DMA((2,)),
            pltpu.SemaphoreType.DMA((2,)),
        ],
        compiler_params=pltpu.CompilerParams(
            collective_id=number, has_side_effects=True, vmem_limit_bytes=60 * 1024 * 1024
        ),
    )(embeddings, ids, slot_row)


def local(embeddings, cluster_ids, cluster_slot):
    rows = embeddings.shape[0]
    clusters = cluster_slot.shape[0]
    ids = cluster_ids.reshape(1, rows)
    slot_row = cluster_slot.reshape(1, clusters)
    quota = clusters // lax.axis_size(("grp", "dev")) * MOST
    best, cent, crowded = exchange(embeddings, ids, slot_row, quota * 3 // 4, 0)

    def whole():
        again = exchange(embeddings, ids, slot_row, quota, 1)
        return again[0], again[1]

    best, cent = lax.cond(crowded[0, 0] > 0, whole, lambda: (best, cent))
    return best.reshape(rows), cent


def solution(mesh):
    in_specs = (P(("grp", "dev"), None), P(("grp", "dev"), None), P())
    out_specs = (P(("grp", "dev")), P(("grp", "dev"), None))
    return jax.shard_map(local, mesh=mesh, in_specs=in_specs, out_specs=out_specs, check_vma=False)
```
